256 devices in a mesh: dp: 8 (over z), section: 16 (over y_hi, x, core), mp: 2 (over y_lo).
Axes of the slice: x: 4, y: 4 (y_hi: 2, y_lo: 2; y = y_hi * 2 + y_lo), z: 8, core: 2. Of those that a mesh axis runs over, the one named last changes fastest.
Arguments:
- stash: bfloat16 [16, 4, 256, 6144], P('section', None, 'dp'), may hold values from -6 to 6
- w_mix: bfloat16 [16, 6144, 6144], P('section', 'dp', 'mp'), may hold values from -0.0390625 to 0.0390625
- top_grad: bfloat16 [4, 256, 6144], P(None, 'dp', 'mp'), may hold values from -6 to 6
- order: int32 [16, 4], P('section'), may hold values from 0 to 3, each once within a row
Outputs:
- input_grad: bfloat16 [16, 4, 256, 6144], P('section', None, 'dp', 'mp')
- grad_mix: bfloat16 [16, 6144, 6144], P('section', 'dp', 'mp')
The draws below stay inside these ranges and needn't reach their ends.
Inputs may be any that keep to these rules, and one draw needn't show every extreme that they name: Each row of order names every micro-batch exactly once.
All inputs are finite; a program needn't handle non-finite values.
Results may differ from the reference program's by a relative error of at most 0.039.
Values may be sent and summed in bfloat16 or wider, within the bound.
A program may use at most 128 MiB of HBM per device.

```python
import math
import jax
import jax.numpy as jnp
from jax import lax

D = 6144
MICRO = 4
ROWS = 256
N_SECTION = 16
N_MP = 2


def steps_of(rng, shape, cuts, low, largest):
    factor_of = 1.0
    for axis_at, shards_of in cuts:
        draws = jax.random.uniform(jax.random.fold_in(jax.random.fold_in(rng, 6), axis_at), (shards_of,), jnp.float32, low / len(cuts), largest / len(cuts))
        factor_of = factor_of * jnp.repeat(jnp.exp(draws), shape[axis_at] // shards_of).reshape((-1,) + (1,) * (len(shape) - 1 - axis_at))
    return factor_of


def gaussian(stream_key, shape, width, most, shards=(), kind=jnp.bfloat16):
    array = width * jax.random.normal(stream_key, shape, jnp.float32)
    if shards:
        array = array * steps_of(stream_key, shape, shards, -0.22, 0.18)
    return jnp.clip(array, -most, most).astype(kind)


def setup_inputs(seed: int = 0) -> dict:
    key_list = jax.random.split(jax.random.key(seed), 5)
    stash = gaussian(key_list[0], (N_SECTION, MICRO, ROWS, D), 1.0, 6.0, ((0, 16), (2, 8)))
    w_mix = gaussian(key_list[1], (N_SECTION, D, D), (4 * D) ** -0.5, 0.0390625, ((0, 16), (1, 8), (2, 2)))
    top_grad = gaussian(key_list[2], (MICRO, ROWS, D), 1.0, 6.0, ((1, 8), (2, 2)))
    order = jax.vmap(lambda own: jax.random.permutation(own, MICRO))(jax.random.split(key_list[3], N_SECTION)).reshape((N_SECTION, MICRO)).astype(jnp.int32)
    return dict(stash=stash, w_mix=w_mix, top_grad=top_grad, order=order)


def gelu_slope(value):
    inner = 0.7978845608 * (value + 0.044715 * value * value * value)
    tangent = jnp.tanh(inner)
    return 0.5 * (1.0 + tangent) + 0.5 * value * (1.0 - tangent * tangent) * 0.7978845608 * (1.0 + 3.0 * 0.044715 * value * value)

def rounded(value):
    return lax.optimization_barrier(value.astype(jnp.bfloat16)).astype(jnp.float32)

def reference(stash, w_mix, top_grad, order):
    scale_factor = 1.0 / math.sqrt(MICRO * ROWS)
    block_unit = D // N_MP
    series = jnp.arange(MICRO, dtype=jnp.int32)
    grads_back = []
    grads_mix = []
    out_grad = top_grad
    for layer in range(N_SECTION - 1, -1, -1):
        match = (order[layer][None, :] == series[:, None]).astype(jnp.int32)
        slots = lax.optimization_barrier(jnp.sum(series[None, :] * match, axis=1)).astype(jnp.int32)
        input_rows = jnp.take(stash[layer], slots, axis=0)
        weight_matrix = w_mix[layer].astype(jnp.float32)
        preactivation_value = jnp.einsum('cuv,vi->cui', input_rows.astype(jnp.float32), weight_matrix)
        hidden_grad = (out_grad.astype(jnp.float32) * gelu_slope(preactivation_value)).astype(jnp.bfloat16)
        wide_hidden_state = hidden_grad.astype(jnp.float32)
        unit_sum = jnp.zeros(out_grad.shape, jnp.float32)
        for part in range(N_MP):
            row_portion = jnp.einsum('ybi,zi->ybz', wide_hidden_state[:, :, part * block_unit:(part + 1) * block_unit], weight_matrix[:, part * block_unit:(part + 1) * block_unit])
            unit_sum = unit_sum + rounded(row_portion)
        new_grad = (out_grad.astype(jnp.float32) + unit_sum).astype(jnp.bfloat16)
        layer_gradient = (scale_factor * jnp.einsum('zgl,zgb->lb', input_rows.astype(jnp.float32), wide_hidden_state)).astype(jnp.bfloat16)
        grads_back.append(new_grad)
        grads_mix.append(layer_gradient)
        out_grad = new_grad
    input_grad = jnp.stack(grads_back[::-1])
    grad_mix = jnp.stack(grads_mix[::-1])
    return (input_grad, grad_mix)
```

```python
import jax
import jax.numpy as jnp
from jax import lax
from jax.experimental import pallas as pl
from jax.experimental.pallas import tpu as pltpu
from jax.sharding import PartitionSpec as P

MESH = pl.DeviceIdType.MESH


def gelu_slope(value):
    inner = 0.7978845608 * (value + 0.044715 * value * value * value)
    tangent = jnp.tanh(inner)
    return 0.5 * (1.0 + tangent) + 0.5 * value * (1.0 - tangent * tangent) * 0.7978845608 * (
        1.0 + 3.0 * 0.044715 * value * value
    )


def relay_kernel(w, slope, top, hidden_out, grad_out, h, inbox, carried, product, in_sem, h_sem, out_sem, copy_sem, flush_sem):
    nz, ns = lax.axis_size("dp"), lax.axis_size("section")
    z, s, m = lax.axis_index("dp"), lax.axis_index("section"), lax.axis_index("mp")
    chunks, rows, columns = h.shape
    block = columns // nz
    quarter = nz // 4
    above, below = lax.rem(s + 1, ns), lax.rem(s + ns - 1, ns)
    is_top = s == ns - 1
    owned = lax.rem(z + nz + quarter * (1 - 2 * m), nz)
    source = m * (nz // 2) + owned // 2
    to_m = z // (nz // 2)
    first = 2 * lax.rem(z, nz // 2) + nz - quarter * (1 - 2 * to_m)
    owners = [lax.rem(first, nz), lax.rem(first + 1, nz)]
    mine = pl.ds(pl.multiple_of(owned * block, block), block)

    barrier = pltpu.get_barrier_semaphore()
    for step in range(1, nz):
        pl.semaphore_signal(barrier, inc=1, device_id=(lax.rem(z + step, nz), s, m), device_id_type=MESH)
    pl.semaphore_signal(barrier, inc=1, device_id=(z, above, m), device_id_type=MESH)
    for part in range(2):
        pl.semaphore_signal(barrier, inc=1, device_id=(source, above, part), device_id_type=MESH)
    pl.semaphore_wait(barrier, nz + 2)

    def received(c):
        pltpu.make_async_copy(inbox.at[c], inbox.at[c], in_sem.at[c]).wait()
        unit_sum = inbox[c, 0].astype(jnp.float32) + inbox[c, 1].astype(jnp.float32)
        return (inbox[c, 2].astype(jnp.float32) + unit_sum).astype(jnp.bfloat16)

    def advance(c, _):
        @pl.when(is_top)
        def _():
            carried[c] = top[c]

        @pl.when(jnp.logical_not(is_top))
        def _():
            value = received(c)
            carried[c] = value
            grad_out[c] = value

        pltpu.make_async_remote_copy(
            src_ref=carried.at[c],
            dst_ref=inbox.at[c, 2],
            send_sem=out_sem.at[c],
            recv_sem=in_sem.at[c],
            device_id=(z, below, m),
            device_id_type=MESH,
        ).start()
        h[c, :, mine] = (carried[c].astype(jnp.float32) * slope[c]).astype(jnp.bfloat16)
        for step in range(1, nz):
            pltpu.make_async_remote_copy(
                src_ref=h.at[c, :, mine],
                dst_ref=h.at[c, :, mine],
                send_sem=copy_sem.at[c],
                recv_sem=h_sem.at[c],
                device_id=(lax.rem(z + step, nz), s, m),
                device_id_type=MESH,
            ).start()
        others = h.at[c, :, pl.ds(0, (nz - 1) * block)]
        pltpu.make_async_copy(others, others, h_sem.at[c]).wait()
        pltpu.make_async_copy(h.at[c], hidden_out.at[c], flush_sem.at[c]).start()
        value = lax.dot_general(
            h[c], w[...], (((1,), (1,)), ((), ())), preferred_element_type=jnp.float32
        ).astype(jnp.bfloat16)
        for part in range(2):
            product[c, part] = value[:, part * block : (part + 1) * block]
            pltpu.make_async_remote_copy(
                src_ref=product.at[c, part],
                dst_ref=inbox.at[c, m],
                send_sem=out_sem.at[c],
                recv_sem=in_sem.at[c],
                device_id=(owners[part], below, to_m),
                device_id_type=MESH,
            ).start()
        return 0

    lax.fori_loop(0, chunks, advance, 0)

    @pl.when(is_top)
    def _():
        def last(c, _):
            grad_out[c] = received(c)
            return 0

        lax.fori_loop(0, chunks, last, 0)

    def drain(c, _):
        others = h.at[c, :, pl.ds(0, (nz - 1) * block)]
        pltpu.make_async_copy(others, others, copy_sem.at[c]).wait()
        pltpu.make_async_copy(inbox.at[c], inbox.at[c], out_sem.at[c]).wait()
        pltpu.make_async_copy(h.at[c], hidden_out.at[c], flush_sem.at[c]).wait()
        return 0

    lax.fori_loop(0, chunks, drain, 0)


def relay(w, slope, top, chunks):
    depth, columns = w.shape
    tokens, block = slope.shape
    rows = tokens // chunks
    hidden, grad = pl.pallas_call(
        relay_kernel,
        out_shape=(
            jax.ShapeDtypeStruct((chunks, rows, columns), jnp.bfloat16),
            jax.ShapeDtypeStruct((chunks, rows, block), jnp.bfloat16),
        ),
        in_specs=[pl.BlockSpec(memory_space=pltpu.VMEM)] * 3,
        out_specs=(pl.BlockSpec(memory_space=pl.ANY), pl.BlockSpec(memory_space=pltpu.VMEM)),
        scratch_shapes=[
            pltpu.VMEM((chunks, rows, columns), jnp.bfloat16),
            pltpu.VMEM((chunks, 3, rows, block), jnp.bfloat16),
            pltpu.VMEM((chunks, rows, block), jnp.bfloat16),
            pltpu.VMEM((chunks, 2, rows, block), jnp.bfloat16),
            pltpu.SemaphoreType.DMA((chunks,)),
            pltpu.SemaphoreType.DMA((chunks,)),
            pltpu.SemaphoreType.DMA((chunks,)),
            pltpu.SemaphoreType.DMA((chunks,)),
            pltpu.SemaphoreType.DMA((chunks,)),
        ],
        compiler_params=pltpu.CompilerParams(
            collective_id=0, has_side_effects=True, vmem_limit_bytes=40 * 1024 * 1024
        ),
        cost_estimate=pl.CostEstimate(
            flops=2 * tokens * depth * columns,
            bytes_accessed=2 * (depth + tokens) * columns,
            transcendentals=0,
        ),
    )(w, slope.reshape(chunks, rows, block), top.reshape(chunks, rows, block))
    return hidden.reshape(tokens, columns), grad.reshape(tokens, block)


def on_device(stash, w_mix, top_grad, order):
    nz, ns = lax.axis_size("dp"), lax.axis_size("section")
    m = lax.axis_index("mp")
    micro, rows = stash.shape[1], stash.shape[2]
    tokens = micro * rows * nz
    weight = w_mix[0]
    depth, half = weight.shape
    block = half // nz
    turn = (nz // 4) * (1 - 2 * m)

    series = jnp.arange(micro, dtype=jnp.int32)
    match = (order[0][None, :] == series[:, None]).astype(jnp.int32)
    slot_table = jnp.sum(series[None, :] * match, axis=1)
    x_own = jnp.take(stash[0], slot_table, axis=0)
    x_cols = lax.all_to_all(x_own, "dp", split_axis=2, concat_axis=1, tiled=True)
    x_flat = x_cols.reshape(tokens, depth)

    turned = jnp.roll(weight.reshape(depth, nz, block), -turn, axis=1)
    partial = jnp.einsum("td,dzb->ztb", x_flat, turned, preferred_element_type=jnp.float32)
    pre = lax.psum_scatter(partial.astype(jnp.bfloat16), "dp", scatter_dimension=0, tiled=False)
    slope = gelu_slope(pre.astype(jnp.float32))

    top_blocks = jnp.roll(top_grad.reshape(micro, rows, nz, block), -turn, axis=2)
    top = lax.all_to_all(top_blocks, "dp", split_axis=2, concat_axis=1, tiled=True).reshape(tokens, block)

    hidden, grad = relay(weight, slope, top, tokens // rows)

    grad = lax.ppermute(grad, "section", [(i, (i + 1) % ns) for i in range(ns)])
    back = lax.all_to_all(grad.reshape(micro, nz, rows, block), "dp", split_axis=1, concat_axis=1, tiled=True)
    back = jnp.roll(back, turn, axis=1)
    input_grad = jnp.transpose(back, (0, 2, 1, 3)).reshape(micro, rows, half)

    grad_mix = tokens ** (-0.5) * lax.dot_general(
        x_flat, hidden, (((0,), (0,)), ((), ())), preferred_element_type=jnp.float32
    )
    return (input_grad[None], grad_mix.astype(jnp.bfloat16)[None])


def solution(mesh):
    in_specs = (
        P("section", None, "dp", None),
        P("section", "dp", "mp"),
        P(None, "dp", "mp"),
        P("section", None),
    )
    out_specs = (P("section", None, "dp", "mp"), P("section", "dp", "mp"))
    return jax.shard_map(
        on_device, mesh=mesh, in_specs=in_specs, out_specs=out_specs, check_vma=False
    )
```

```python
import jax
import jax.numpy as jnp
from jax import lax
from jax.experimental import pallas as pl
from jax.experimental.pallas import tpu as pltpu
from jax.sharding import PartitionSpec as P

MESH = pl.DeviceIdType.MESH
LAG = 1


def gelu_slope(value):
    inner = 0.7978845608 * (value + 0.044715 * value * value * value)
    tangent = jnp.tanh(inner)
    return 0.5 * (1.0 + tangent) + 0.5 * value * (1.0 - tangent * tangent) * 0.7978845608 * (
        1.0 + 3.0 * 0.044715 * value * value
    )


def send(src, dst, send_sem, recv_sem, device):
    pltpu.make_async_remote_copy(
        src_ref=src, dst_ref=dst, send_sem=send_sem, recv_sem=recv_sem, device_id=device, device_id_type=MESH
    ).start()


def await_bytes(ref, sem):
    pltpu.make_async_copy(ref, ref, sem).wait()


def turn_of(m, nz):
    return (nz // 4) * (1 - 2 * m)


def prepare_kernel(x_own, w, x_out, slope, x, ring, sent, x_sem, x_sent, y_sem, y_sent, own_sem, ring_sem, ring_sent, flush_sem):
    nz = lax.axis_size("dp")
    z, s, m = lax.axis_index("dp"), lax.axis_index("section"), lax.axis_index("mp")
    micro, _, rows, depth = x.shape
    block = slope.shape[-1]
    pair = micro // 2
    steps = sorted(range(1, nz), key=lambda k: min(k, nz - k))
    partner = (z, s, 1 - m)
    mine = pl.ds(m * pair, pair)
    theirs = pl.ds((1 - m) * pair, pair)

    barrier = pltpu.get_barrier_semaphore()
    for step in steps:
        pl.semaphore_signal(barrier, inc=1, device_id=(lax.rem(z + step, nz), s, m), device_id_type=MESH)
    pl.semaphore_signal(barrier, inc=1, device_id=partner, device_id_type=MESH)
    pl.semaphore_wait(barrier, nz)

    def piece(owner):
        return x_own.at[mine, :, pl.ds(pl.multiple_of(owner * depth, depth), depth)]

    own = pltpu.make_async_copy(piece(z), x.at[mine, z], own_sem)
    own.start()
    for step in steps[::-1]:
        owner = lax.rem(z + step, nz)
        send(piece(owner), x.at[mine, z], x_sent.at[step], x_sem.at[step], (owner, s, m))
    send(piece(z), x.at[mine, z], y_sent.at[0], y_sem.at[0], partner)
    for step in steps:
        origin = lax.rem(z + nz - step, nz)
        await_bytes(x.at[mine, origin], x_sem.at[step])
        send(x.at[mine, origin], x.at[mine, origin], y_sent.at[step], y_sem.at[step], partner)
    own.wait()
    for step in range(nz):
        await_bytes(x.at[theirs, lax.rem(z + nz - step, nz)], y_sem.at[step])
    flush = pltpu.make_async_copy(x, x_out, flush_sem)
    flush.start()

    def partial(t, q):
        owner = lax.rem(z + 2 * nz - 1 - t, nz) if q < pair else lax.rem(z + 1 + t, nz)
        at = lax.rem(owner + nz + turn_of(m, nz), nz) * block
        return jnp.dot(
            x[q].reshape(nz * rows, depth),
            w[:, pl.ds(pl.multiple_of(at, block), block)],
            preferred_element_type=jnp.float32,
        )

    def pass_on(t, q, value):
        sent[t, q] = value.astype(jnp.bfloat16)
        to = lax.rem(z + 1, nz) if q < pair else lax.rem(z + nz - 1, nz)
        send(sent.at[t, q], ring.at[t, q], ring_sent.at[t, q], ring_sem.at[t, q], (to, s, m))

    order = [q // 2 + (q % 2) * pair for q in range(micro)]
    for q in order:
        pass_on(0, q, partial(0, q))

    def step_of(t, _):
        for q in order:
            value = partial(t, q)
            await_bytes(ring.at[t - 1, q], ring_sem.at[t - 1, q])
            pass_on(t, q, value + ring[t - 1, q].astype(jnp.float32))
        return 0

    lax.fori_loop(1, nz - 1, step_of, 0)
    for q in order:
        value = partial(nz - 1, q)
        await_bytes(ring.at[nz - 2, q], ring_sem.at[nz - 2, q])
        slope[q] = gelu_slope(value + ring[nz - 2, q].astype(jnp.float32))

    flush.wait()
    for step in steps:
        await_bytes(x.at[mine, z], x_sent.at[step])
    for step in range(nz):
        await_bytes(x.at[mine, z], y_sent.at[step])

    def drain(t, _):
        for q in range(micro):
            await_bytes(sent.at[t, q], ring_sent.at[t, q])
        return 0

    lax.fori_loop(0, nz - 1, drain, 0)


def prepare(x_own, w, cid=0):
    nz = lax.axis_size("dp")
    micro, rows, width = x_own.shape
    depth, half = w.shape
    block = half // nz
    dma = pltpu.SemaphoreType.DMA
    return pl.pallas_call(
        prepare_kernel,
        out_shape=(
            jax.ShapeDtypeStruct((micro, nz, rows, depth), jnp.bfloat16),
            jax.ShapeDtypeStruct((micro, nz * rows, block), jnp.float32),
        ),
        in_specs=[pl.BlockSpec(memory_space=pltpu.VMEM)] * 2,
        out_specs=(pl.BlockSpec(memory_space=pl.ANY), pl.BlockSpec(memory_space=pltpu.VMEM)),
        scratch_shapes=[
            pltpu.VMEM((micro, nz, rows, depth), jnp.bfloat16),
            pltpu.VMEM((nz - 1, micro, nz * rows, block), jnp.bfloat16),
            pltpu.VMEM((nz - 1, micro, nz * rows, block), jnp.bfloat16),
            dma((nz,)),
            dma((nz,)),
            dma((nz,)),
            dma((nz,)),
            dma,
            dma((nz - 1, micro)),
            dma((nz - 1, micro)),
            dma,
        ],
        compiler_params=pltpu.CompilerParams(
            collective_id=cid, has_side_effects=True, vmem_limit_bytes=44 * 1024 * 1024
        ),
        cost_estimate=pl.CostEstimate(
            flops=2 * micro * nz * rows * depth * half,
            bytes_accessed=2 * depth * half,
            transcendentals=0,
        ),
    )(x_own, w)


def relay_kernel(w, slope, top, hidden_out, grad_out, h, inbox, carried, product, back, in_sem, h_sem, out_sem, copy_sem, flush_sem, back_sent, back_sem, top_sent, top_sem):
    nz, ns = lax.axis_size("dp"), lax.axis_size("section")
    z, s, m = lax.axis_index("dp"), lax.axis_index("section"), lax.axis_index("mp")
    chunks, rows, columns = h.shape
    micro = chunks // nz
    block = columns // nz
    above, below = lax.rem(s + 1, ns), lax.rem(s + ns - 1, ns)
    is_top = s == ns - 1

    def place(owner):
        return pl.ds(pl.multiple_of(lax.rem(owner + nz + turn_of(m, nz), nz) * block, block), block)

    source = m * (nz // 2) + lax.rem(z + nz + turn_of(m, nz), nz) // 2
    to_m = z // (nz // 2)
    first = 2 * lax.rem(z, nz // 2) + nz - turn_of(to_m, nz)
    owners = [lax.rem(first, nz), lax.rem(first + 1, nz)]
    mine = place(z)

    barrier = pltpu.get_barrier_semaphore()
    for step in range(1, nz):
        pl.semaphore_signal(barrier, inc=1, device_id=(lax.rem(z + step, nz), s, m), device_id_type=MESH)
    for step in range(nz):
        pl.semaphore_signal(barrier, inc=1, device_id=(lax.rem(z + step, nz), below, m), device_id_type=MESH)
    pl.semaphore_signal(barrier, inc=1, device_id=(z, above, m), device_id_type=MESH)
    for part in range(2):
        pl.semaphore_signal(barrier, inc=1, device_id=(source, above, part), device_id_type=MESH)
    pl.semaphore_wait(barrier, 2 * nz + 2)

    @pl.when(is_top)
    def _():
        def spread(q, _):
            for step in range(1, nz):
                owner = lax.rem(z + step, nz)
                send(top.at[q, :, place(owner)], carried.at[q * nz + z], top_sent.at[q], top_sem.at[q], (owner, s, m))
            carried[q * nz + z] = top[q, :, mine]
            return 0

        lax.fori_loop(0, micro, spread, 0)

    def received(c):
        await_bytes(inbox.at[c], in_sem.at[c])
        unit_sum = inbox[c, 0].astype(jnp.float32) + inbox[c, 1].astype(jnp.float32)
        return (inbox[c, 2].astype(jnp.float32) + unit_sum).astype(jnp.bfloat16)

    def send_back(c):
        q, d = c // nz, lax.rem(c, nz)
        send(carried.at[c], back.at[q, :, mine], back_sent, back_sem, (d, above, m))

    def share(c, owner, step, sem):
        at = place(owner)
        send(h.at[c, :, at], h.at[c, :, at], copy_sem.at[c], sem.at[c], (lax.rem(z + nz + step, nz), s, m))

    def publish(c):
        @pl.when(is_top)
        def _():
            @pl.when(lax.rem(c, nz) == 0)
            def _():
                await_bytes(carried.at[pl.ds(0, nz - 1)], top_sem.at[c // nz])

        @pl.when(jnp.logical_not(is_top))
        def _():
            carried[c] = received(c)

        h[c, :, mine] = (carried[c].astype(jnp.float32) * slope[c]).astype(jnp.bfloat16)
        for step in sorted(range(1, nz), key=lambda k: -min(k, nz - k)):
            share(c, z, step, h_sem)
        send(carried.at[c], inbox.at[c, 2], out_sem.at[c], in_sem.at[c], (z, below, m))

    def multiply(c):
        await_bytes(h.at[c, :, pl.ds(0, (nz - 1) * block)], h_sem.at[c])
        value = jnp.dot(h[c], w[...], preferred_element_type=jnp.float32).astype(jnp.bfloat16)
        for part in range(2):
            product[c, part] = value[:, part * block : (part + 1) * block]
            send(product.at[c, part], inbox.at[c, m], out_sem.at[c], in_sem.at[c], (owners[part], below, to_m))
        pltpu.make_async_copy(h.at[c], hidden_out.at[c], flush_sem.at[c]).start()

    def advance(i, _):
        @pl.when(i < chunks)
        def _():
            publish(i)

        @pl.when(i >= LAG)
        def _():
            multiply(i - LAG)

        return 0

    lax.fori_loop(0, chunks + LAG, advance, 0)

    @pl.when(jnp.logical_not(is_top))
    def _():
        def later(c, _):
            send_back(c)
            return 0

        lax.fori_loop(0, chunks, later, 0)

    @pl.when(is_top)
    def _():
        for q in range(micro):
            await_bytes(carried.at[pl.ds(0, nz - 1)], top_sent.at[q])

        def last(c, _):
            await_bytes(inbox.at[c], out_sem.at[c])
            carried[c] = received(c)
            send_back(c)
            return 0

        lax.fori_loop(0, chunks, last, 0)

    def drain(c, _):
        await_bytes(h.at[c, :, pl.ds(0, (nz - 1) * block)], copy_sem.at[c])

        @pl.when(jnp.logical_not(is_top))
        def _():
            await_bytes(inbox.at[c], out_sem.at[c])

        await_bytes(h.at[c], flush_sem.at[c])
        return 0

    lax.fori_loop(0, chunks, drain, 0)
    await_bytes(back, back_sem)
    grad_out[...] = back[...]
    await_bytes(back, back_sent)


def relay(w, slope, top, cid=1):
    columns, depth = w.shape
    micro, rows, _ = top.shape
    block = slope.shape[-1]
    tokens = slope.shape[0] * slope.shape[1]
    chunks = tokens // rows
    dma = pltpu.SemaphoreType.DMA
    return pl.pallas_call(
        relay_kernel,
        out_shape=(
            jax.ShapeDtypeStruct((chunks, rows, columns), jnp.bfloat16),
            jax.ShapeDtypeStruct((micro, rows, columns), jnp.bfloat16),
        ),
        in_specs=[pl.BlockSpec(memory_space=pltpu.VMEM)] * 3,
        out_specs=(pl.BlockSpec(memory_space=pl.ANY), pl.BlockSpec(memory_space=pltpu.VMEM)),
        scratch_shapes=[
            pltpu.VMEM((chunks, rows, columns), jnp.bfloat16),
            pltpu.VMEM((chunks, 3, rows, block), jnp.bfloat16),
            pltpu.VMEM((chunks, rows, block), jnp.bfloat16),
            pltpu.VMEM((chunks, 2, rows, block), jnp.bfloat16),
            pltpu.VMEM((micro, rows, columns), jnp.bfloat16),
            dma((chunks,)),
            dma((chunks,)),
            dma((chunks,)),
            dma((chunks,)),
            dma((chunks,)),
            dma,
            dma,
            dma((micro,)),
            dma((micro,)),
        ],
        compiler_params=pltpu.CompilerParams(
            collective_id=cid, has_side_effects=True, vmem_limit_bytes=40 * 1024 * 1024
        ),
        cost_estimate=pl.CostEstimate(
            flops=2 * tokens * depth * columns,
            bytes_accessed=2 * (depth + tokens) * columns,
            transcendentals=0,
        ),
    )(w, slope.reshape(chunks, rows, block), top)


def on_device(stash, w_mix, top_grad, order):
    micro = stash.shape[1]
    weight = w_mix[0]
    depth, half = weight.shape

    series = jnp.arange(micro, dtype=jnp.int32)
    match = (order[0][None, :] == series[:, None]).astype(jnp.int32)
    slot_table = jnp.sum(series[None, :] * match, axis=1)
    x_own = jnp.take(stash[0], slot_table, axis=0)
    x, slope = prepare(x_own, weight)
    x = x.reshape(-1, depth)
    hidden, input_grad = relay(weight.T, slope, top_grad)
    grad_mix = x.shape[0] ** (-0.5) * lax.dot_general(
        x, hidden.reshape(-1, half), (((0,), (0,)), ((), ())), preferred_element_type=jnp.float32
    )
    return (input_grad[None], grad_mix.astype(jnp.bfloat16)[None])


def solution(mesh):
    in_specs = (
        P("section", None, "dp", None),
        P("section", "dp", "mp"),
        P(None, "dp", "mp"),
        P("section", None),
    )
    out_specs = (P("section", None, "dp", "mp"), P("section", "dp", "mp"))
    return jax.shard_map(
        on_device, mesh=mesh, in_specs=in_specs, out_specs=out_specs, check_vma=False
    )
```

```python
import jax
import jax.numpy as jnp
from jax import lax
from jax.experimental import pallas as pl
from jax.experimental.pallas import tpu as pltpu
from jax.sharding import PartitionSpec as P

MESH = pl.DeviceIdType.MESH
LAG = 1


def gelu_slope(value):
    inner = 0.7978845608 * (value + 0.044715 * value * value * value)
    tangent = jnp.tanh(inner)
    return 0.5 * (1.0 + tangent) + 0.5 * value * (1.0 - tangent * tangent) * 0.7978845608 * (
        1.0 + 3.0 * 0.044715 * value * value
    )


def send(src, dst, send_sem, recv_sem, device):
    pltpu.make_async_remote_copy(
        src_ref=src, dst_ref=dst, send_sem=send_sem, recv_sem=recv_sem, device_id=device, device_id_type=MESH
    ).start()


def await_bytes(ref, sem):
    pltpu.make_async_copy(ref, ref, sem).wait()


def turn_of(m, nz):
    return (nz // 4) * (1 - 2 * m)


def layer_kernel(x_own, w, top, x_out, hidden_out, grad_out, x, ring, sent, w_t, slope_in, h, inbox, carried, shared, product, slope, back, in_sem, h_sem, out_sem, copy_sem, flush_sem, back_sent, back_sem, top_sent, top_sem, slope_sent, slope_sem, x_sem, x_sent, y_sem, y_sent, own_sem, ring_sem, ring_sent, x_flush_sem):
    nz, ns = lax.axis_size("dp"), lax.axis_size("section")
    z, s, m = lax.axis_index("dp"), lax.axis_index("section"), lax.axis_index("mp")
    chunks, rows, columns = h.shape
    micro = chunks // nz
    block = columns // nz
    depth = x.shape[-1]
    pair = micro // 2
    steps = sorted(range(1, nz), key=lambda k: min(k, nz - k))
    partner = (z, s, 1 - m)
    kept = pl.ds(m * pair, pair)
    given = pl.ds((1 - m) * pair, pair)
    above, below = lax.rem(s + 1, ns), lax.rem(s + ns - 1, ns)
    is_top = s == ns - 1

    to_m = z // (nz // 2)
    own = 2 * lax.rem(z, nz // 2) + m
    in_column = to_m == m

    def place(number):
        return pl.ds(pl.multiple_of(number * block, block), block)

    def owner_of(number):
        return (m * (nz // 2) + number // 2, s, lax.rem(number, 2))

    def each_other(step, call):
        if step:
            call(step)
        else:
            pl.when(jnp.logical_not(in_column))(lambda: call(step))

    barrier = pltpu.get_barrier_semaphore()

    def greet(device):
        pl.semaphore_signal(barrier, inc=1, device_id=device, device_id_type=MESH)

    for step in range(nz):
        each_other(step, lambda k: greet(owner_of(lax.rem(own + k, nz))))
        each_other(step, lambda k: greet((lax.rem(z + k, nz), s, to_m)))
        greet((m * (nz // 2) + step // 2, below, step % 2))
    for step in steps:
        greet((lax.rem(z + step, nz), s, m))
    greet(partner)
    greet((z, above, 0))
    greet((z, above, 1))
    pl.when(in_column)(lambda: pl.semaphore_wait(barrier, 4 * nz))
    pl.when(jnp.logical_not(in_column))(lambda: pl.semaphore_wait(barrier, 4 * nz + 2))

    mine = place(own)
    number = lax.rem(z + nz + turn_of(m, nz), nz)
    at_home = jnp.logical_and(in_column, number == own)

    def piece(owner):
        return x_own.at[kept, :, pl.ds(pl.multiple_of(owner * depth, depth), depth)]

    own_copy = pltpu.make_async_copy(piece(z), x.at[kept, z], own_sem)
    own_copy.start()
    for step in steps[::-1]:
        owner = lax.rem(z + step, nz)
        send(piece(owner), x.at[kept, z], x_sent.at[step], x_sem.at[step], (owner, s, m))
    send(piece(z), x.at[kept, z], y_sent.at[0], y_sem.at[0], partner)

    @pl.when(is_top)
    def _():
        def spread(q, _):
            def give(step):
                to = lax.rem(own + step, nz)
                send(top.at[q, :, place(to)], carried.at[q * nz + z], top_sent.at[q], top_sem.at[q], owner_of(to))

            for step in range(nz):
                each_other(step, give)

            @pl.when(in_column)
            def _():
                carried[q * nz + z] = top[q, :, mine]

            return 0

        lax.fori_loop(0, micro, spread, 0)

    def transpose(k, _):
        at = pl.ds(pl.multiple_of(k * block, block), block)
        w_t[at, :] = w[:, at].T
        return 0

    lax.fori_loop(0, nz, transpose, 0)

    for step in steps:
        origin = lax.rem(z + nz - step, nz)
        await_bytes(x.at[kept, origin], x_sem.at[step])
        send(x.at[kept, origin], x.at[kept, origin], y_sent.at[step], y_sem.at[step], partner)
    own_copy.wait()
    for step in range(nz):
        await_bytes(x.at[given, lax.rem(z + nz - step, nz)], y_sem.at[step])
    x_flush = pltpu.make_async_copy(x, x_out, x_flush_sem)
    x_flush.start()

    def partial(t, q):
        owner = lax.rem(z + 2 * nz - 1 - t, nz) if q < pair else lax.rem(z + 1 + t, nz)
        at = lax.rem(owner + nz + turn_of(m, nz), nz) * block
        return jnp.dot(
            x[q].reshape(nz * rows, depth),
            w[:, pl.ds(pl.multiple_of(at, block), block)],
            preferred_element_type=jnp.float32,
        )

    def pass_on(t, q, value):
        sent[t, q] = value.astype(jnp.bfloat16)
        to = lax.rem(z + 1, nz) if q < pair else lax.rem(z + nz - 1, nz)
        send(sent.at[t, q], ring.at[t, q], ring_sent.at[t, q], ring_sem.at[t, q], (to, s, m))

    def local_slope(q):
        part = pl.ds(q * nz, nz)
        return pltpu.make_async_copy(slope_in.at[part], slope.at[part], slope_sem.at[q])

    order = [q // 2 + (q % 2) * pair for q in range(micro)]
    for q in order:
        pass_on(0, q, partial(0, q))

    def step_of(t, _):
        for q in order:
            value = partial(t, q)
            await_bytes(ring.at[t - 1, q], ring_sem.at[t - 1, q])
            pass_on(t, q, value + ring[t - 1, q].astype(jnp.float32))
        return 0

    lax.fori_loop(1, nz - 1, step_of, 0)
    for q in order:
        value = partial(nz - 1, q)
        await_bytes(ring.at[nz - 2, q], ring_sem.at[nz - 2, q])
        value = gelu_slope(value + ring[nz - 2, q].astype(jnp.float32)).astype(jnp.bfloat16)
        part = pl.ds(q * nz, nz)
        slope_in[part] = value.reshape(nz, rows, block)
        pl.when(at_home)(lambda: local_slope(q).start())

        @pl.when(jnp.logical_not(at_home))
        def _():
            send(slope_in.at[part], slope.at[part], slope_sent.at[q], slope_sem.at[q], owner_of(number))

    def await_blocks(ref, sem):
        pl.when(in_column)(lambda: await_bytes(ref.at[pl.ds(0, nz - 1)], sem))
        pl.when(jnp.logical_not(in_column))(lambda: await_bytes(ref.at[pl.ds(0, nz)], sem))

    def received(c):
        await_bytes(inbox.at[c], in_sem.at[c])
        return (inbox[c, 0].astype(jnp.float32) + inbox[c, 1].astype(jnp.float32)).astype(jnp.bfloat16)

    def send_back(c):
        q, d = c // nz, lax.rem(c, nz)
        send(carried.at[c], back.at[q, :, mine], back_sent, back_sem, (d, above, to_m))

    def publish(c):
        @pl.when(lax.rem(c, nz) == 0)
        def _():
            await_bytes(slope.at[pl.ds(c, nz)], slope_sem.at[c // nz])

            @pl.when(is_top)
            def _():
                await_blocks(carried, top_sem.at[c // nz])

        @pl.when(jnp.logical_not(is_top))
        def _():
            carried[c] = received(c)

        value = (carried[c].astype(jnp.float32) * slope[c].astype(jnp.float32)).astype(jnp.bfloat16)
        shared[c] = value

        def share(step):
            send(shared.at[c], h.at[c, :, mine], copy_sem.at[c], h_sem.at[c, own // 2], (lax.rem(z + step, nz), s, to_m))

        for step in sorted(range(nz), key=lambda k: -min(k, nz - k)):
            each_other(step, share)

        @pl.when(in_column)
        def _():
            h[c, :, mine] = value

    sources = nz // 2
    nearest = jnp.where(in_column, z, z + 1)

    def multiply(c):
        total = None
        for k in range(sources):
            near = lax.rem(nearest + k, sources)
            if k:
                await_bytes(shared.at[pl.ds(0, 2)], h_sem.at[c, near])
            else:
                pl.when(in_column)(lambda: await_bytes(shared.at[0], h_sem.at[c, near]))
                pl.when(jnp.logical_not(in_column))(lambda: await_bytes(shared.at[pl.ds(0, 2)], h_sem.at[c, near]))
            at = pl.ds(pl.multiple_of(near * 2 * block, 2 * block), 2 * block)
            term = jnp.dot(h[c, :, at], w_t[at, :], preferred_element_type=jnp.float32)
            total = term if total is None else total + term
        for part in range(2):
            value = total[:, part * block : (part + 1) * block]
            value = value + jnp.where(m == part, carried[c].astype(jnp.float32), 0.0)
            product[c, part] = value.astype(jnp.bfloat16)
            send(product.at[c, part], inbox.at[c, m], out_sem.at[c], in_sem.at[c], (z, below, part))
        pltpu.make_async_copy(h.at[c], hidden_out.at[c], flush_sem.at[c]).start()

    def advance(i, _):
        @pl.when(i < chunks)
        def _():
            publish(i)

        @pl.when(i >= LAG)
        def _():
            multiply(i - LAG)

        return 0

    lax.fori_loop(0, chunks + LAG, advance, 0)

    @pl.when(jnp.logical_not(is_top))
    def _():
        def later(c, _):
            send_back(c)
            return 0

        lax.fori_loop(0, chunks, later, 0)

    @pl.when(is_top)
    def _():
        def last(c, _):
            await_bytes(inbox.at[c], out_sem.at[c])
            carried[c] = received(c)
            send_back(c)
            return 0

        lax.fori_loop(0, chunks, last, 0)
        for q in range(micro):
            await_blocks(shared, top_sent.at[q])

    def drain(c, _):
        await_blocks(shared, copy_sem.at[c])

        @pl.when(jnp.logical_not(is_top))
        def _():
            await_bytes(inbox.at[c], out_sem.at[c])

        await_bytes(h.at[c], flush_sem.at[c])
        return 0

    lax.fori_loop(0, chunks, drain, 0)

    @pl.when(jnp.logical_not(at_home))
    def _():
        for q in range(micro):
            await_bytes(slope.at[pl.ds(0, nz)], slope_sent.at[q])

    x_flush.wait()
    for step in steps:
        await_bytes(x.at[kept, z], x_sent.at[step])
    for step in range(nz):
        await_bytes(x.at[kept, z], y_sent.at[step])

    def drain_ring(t, _):
        for q in range(micro):
            await_bytes(sent.at[t, q], ring_sent.at[t, q])
        return 0

    lax.fori_loop(0, nz - 1, drain_ring, 0)

    await_bytes(back, back_sem)
    grad_out[...] = back[...]
    await_bytes(back, back_sent)


def layers(x_own, w, top, cid=0):
    nz = lax.axis_size("dp")
    micro, rows, _ = x_own.shape
    depth, columns = w.shape
    block = columns // nz
    chunks = micro * nz
    dma = pltpu.SemaphoreType.DMA

    def buffer(*shape):
        return pltpu.VMEM(shape, jnp.bfloat16)

    return pl.pallas_call(
        layer_kernel,
        out_shape=(
            jax.ShapeDtypeStruct((micro, nz, rows, depth), jnp.bfloat16),
            jax.ShapeDtypeStruct((chunks, rows, columns), jnp.bfloat16),
            jax.ShapeDtypeStruct((micro, rows, columns), jnp.bfloat16),
        ),
        in_specs=[pl.BlockSpec(memory_space=pltpu.VMEM)] * 3,
        out_specs=(
            pl.BlockSpec(memory_space=pl.ANY),
            pl.BlockSpec(memory_space=pl.ANY),
            pl.BlockSpec(memory_space=pltpu.VMEM),
        ),
        scratch_shapes=[
            buffer(micro, nz, rows, depth),
            buffer(nz - 1, micro, nz * rows, block),
            buffer(nz - 1, micro, nz * rows, block),
            buffer(columns, depth),
            buffer(chunks, rows, block),
            buffer(chunks, rows, columns),
            buffer(chunks, 2, rows, block),
            buffer(chunks, rows, block),
            buffer(chunks, rows, block),
            buffer(chunks, 2, rows, block),
            buffer(chunks, rows, block),
            buffer(micro, rows, columns),
            dma((chunks,)),
            dma((chunks, nz // 2)),
            dma((chunks,)),
            dma((chunks,)),
            dma((chunks,)),
            dma,
            dma,
            dma((micro,)),
            dma((micro,)),
            dma((micro,)),
            dma((micro,)),
            dma((nz,)),
            dma((nz,)),
            dma((nz,)),
            dma((nz,)),
            dma,
            dma((nz - 1, micro)),
            dma((nz - 1, micro)),
            dma,
        ],
        compiler_params=pltpu.CompilerParams(
            collective_id=cid, has_side_effects=True, vmem_limit_bytes=56 * 1024 * 1024
        ),
        cost_estimate=pl.CostEstimate(
            flops=4 * chunks * rows * depth * columns,
            bytes_accessed=4 * depth * columns,
            transcendentals=0,
        ),
    )(x_own, w, top)


def on_device(stash, w_mix, top_grad, order):
    micro = stash.shape[1]
    weight = w_mix[0]
    depth, half = weight.shape

    series = jnp.arange(micro, dtype=jnp.int32)
    match = (order[0][None, :] == series[:, None]).astype(jnp.int32)
    slot_table = jnp.sum(series[None, :] * match, axis=1)
    x_own = jnp.take(stash[0], slot_table, axis=0)
    x, hidden, input_grad = layers(x_own, weight, top_grad)
    x = x.reshape(-1, depth)
    grad_mix = x.shape[0] ** (-0.5) * lax.dot_general(
        x, hidden.reshape(-1, half), (((0,), (0,)), ((), ())), preferred_element_type=jnp.float32
    )
    return (input_grad[None], grad_mix.astype(jnp.bfloat16)[None])


def solution(mesh):
    in_specs = (
        P("section", None, "dp", None),
        P("section", "dp", "mp"),
        P(None, "dp", "mp"),
        P("section", None),
    )
    out_specs = (P("section", None, "dp", "mp"), P("section", "dp", "mp"))
    return jax.shard_map(
        on_device, mesh=mesh, in_specs=in_specs, out_specs=out_specs, check_vma=False
    )
```

```python
import jax
import jax.numpy as jnp
from jax import lax
from jax.experimental import pallas as pl
from jax.experimental.pallas import tpu as pltpu
from jax.sharding import PartitionSpec as P

MESH = pl.DeviceIdType.MESH
LAG = 1


def gelu_slope(value):
    inner = 0.7978845608 * (value + 0.044715 * value * value * value)
    tangent = jnp.tanh(inner)
    return 0.5 * (1.0 + tangent) + 0.5 * value * (1.0 - tangent * tangent) * 0.7978845608 * (
        1.0 + 3.0 * 0.044715 * value * value
    )


def send(src, dst, send_sem, recv_sem, device):
    pltpu.make_async_remote_copy(
        src_ref=src, dst_ref=dst, send_sem=send_sem, recv_sem=recv_sem, device_id=device, device_id_type=MESH
    ).start()


def await_bytes(ref, sem):
    pltpu.make_async_copy(ref, ref, sem).wait()


def turn_of(m, nz):
    return (nz // 4) * (1 - 2 * m)


def layer_kernel(x_own, w, top, mix_out, grad_out, x, x_t, mix, ring, sent, w_t, slope_in, h, inbox, carried, shared, product, slope, back, in_sem, h_sem, out_sem, copy_sem, mix_sem, back_sent, back_sem, top_sent, top_sem, slope_sent, slope_sem, x_sem, x_sent, y_sem, y_sent, own_sem, ring_sem, ring_sent):
    nz, ns = lax.axis_size("dp"), lax.axis_size("section")
    z, s, m = lax.axis_index("dp"), lax.axis_index("section"), lax.axis_index("mp")
    chunks, rows, columns = h.shape
    micro = chunks // nz
    block = columns // nz
    depth = x.shape[-1]
    pair = micro // 2
    steps = sorted(range(1, nz), key=lambda k: min(k, nz - k))
    partner = (z, s, 1 - m)
    above, below = lax.rem(s + 1, ns), lax.rem(s + ns - 1, ns)
    is_top = s == ns - 1

    to_m = z // (nz // 2)
    own = 2 * lax.rem(z, nz // 2) + m
    in_column = to_m == m

    def place(number):
        return pl.ds(pl.multiple_of(number * block, block), block)

    def owner_of(number):
        return (m * (nz // 2) + number // 2, s, lax.rem(number, 2))

    def each_other(step, call):
        if step:
            call(step)
        else:
            pl.when(jnp.logical_not(in_column))(lambda: call(step))

    barrier = pltpu.get_barrier_semaphore()

    def greet(device):
        pl.semaphore_signal(barrier, inc=1, device_id=device, device_id_type=MESH)

    for step in range(nz):
        each_other(step, lambda k: greet(owner_of(lax.rem(own + k, nz))))
        each_other(step, lambda k: greet((lax.rem(z + k, nz), s, to_m)))
        greet((m * (nz // 2) + step // 2, below, step % 2))
    for step in steps:
        greet((lax.rem(z + step, nz), s, m))
    greet(partner)
    greet((z, above, 0))
    greet((z, above, 1))
    pl.when(in_column)(lambda: pl.semaphore_wait(barrier, 4 * nz))
    pl.when(jnp.logical_not(in_column))(lambda: pl.semaphore_wait(barrier, 4 * nz + 2))

    mine = place(own)
    number = lax.rem(z + nz + turn_of(m, nz), nz)
    at_home = jnp.logical_and(in_column, number == own)

    batches = [(m if k < pair else 1 - m) * pair + k % pair for k in range(micro)]

    def piece(k, owner):
        return x_own.at[batches[k], :, pl.ds(pl.multiple_of(owner * depth, depth), depth)]

    def own_copy(k):
        return pltpu.make_async_copy(piece(k, z), x.at[batches[k], z], own_sem.at[k])

    for k in range(pair):
        own_copy(k).start()
        for step in steps[::-1]:
            owner = lax.rem(z + step, nz)
            send(piece(k, owner), x.at[batches[k], z], x_sent.at[k, step], x_sem.at[k, step], (owner, s, m))
        send(piece(k, z), x.at[batches[k], z], y_sent.at[k, 0], y_sem.at[k, 0], partner)

    @pl.when(is_top)
    def _():
        def spread(q, _):
            def give(step):
                to = lax.rem(own + step, nz)
                send(top.at[q, :, place(to)], carried.at[q * nz + z], top_sent.at[q], top_sem.at[q], owner_of(to))

            for step in range(nz):
                each_other(step, give)

            @pl.when(in_column)
            def _():
                carried[q * nz + z] = top[q, :, mine]

            return 0

        lax.fori_loop(0, micro, spread, 0)

    def transpose(k, _):
        at = pl.ds(pl.multiple_of(k * block, block), block)
        w_t[at, :] = w[:, at].T
        return 0

    lax.fori_loop(0, nz, transpose, 0)

    def partial(t, k):
        owner = lax.rem(z + nz + 1 + t, nz) if k % 2 else lax.rem(z + 2 * nz - 1 - t, nz)
        at = lax.rem(owner + nz + turn_of(m, nz), nz) * block
        return jnp.dot(
            x[batches[k]].reshape(nz * rows, depth),
            w[:, pl.ds(pl.multiple_of(at, block), block)],
            preferred_element_type=jnp.float32,
        )

    def pass_on(t, k, value):
        sent[t, k] = value.astype(jnp.bfloat16)
        to = lax.rem(z + nz - 1, nz) if k % 2 else lax.rem(z + 1, nz)
        send(sent.at[t, k], ring.at[t, k], ring_sent.at[t, k], ring_sem.at[t, k], (to, s, m))

    for k in range(pair):
        own_copy(k).wait()
        for step in steps:
            here = x.at[batches[k], lax.rem(z + nz - step, nz)]
            await_bytes(here, x_sem.at[k, step])
            send(here, here, y_sent.at[k, step], y_sem.at[k, step], partner)
        pass_on(0, k, partial(0, k))
    for k in range(pair, micro):
        for step in range(nz):
            await_bytes(x.at[batches[k], lax.rem(z + nz - step, nz)], y_sem.at[k - pair, step])
        pass_on(0, k, partial(0, k))

    def step_of(t, _):
        @pl.when(t <= 2)
        def _():
            for half in range(pair):
                q = (t - 1) * pair + half
                x_t[:, pl.ds(pl.multiple_of(q * nz * rows, nz * rows), nz * rows)] = x[q].reshape(nz * rows, depth).T

        for k in range(micro):
            value = partial(t, k)
            await_bytes(ring.at[t - 1, k], ring_sem.at[t - 1, k])
            pass_on(t, k, value + ring[t - 1, k].astype(jnp.float32))
        return 0

    lax.fori_loop(1, nz - 1, step_of, 0)

    def local_slope(part, q):
        return pltpu.make_async_copy(slope_in.at[part], slope.at[part], slope_sem.at[q])

    for k in range(micro):
        value = partial(nz - 1, k)
        await_bytes(ring.at[nz - 2, k], ring_sem.at[nz - 2, k])
        value = gelu_slope(value + ring[nz - 2, k].astype(jnp.float32)).astype(jnp.bfloat16)
        q = batches[k]
        part = pl.ds(q * nz, nz)
        slope_in[part] = value.reshape(nz, rows, block)
        pl.when(at_home)(lambda: local_slope(part, q).start())

        @pl.when(jnp.logical_not(at_home))
        def _():
            send(slope_in.at[part], slope.at[part], slope_sent.at[q], slope_sem.at[q], owner_of(number))

    def await_blocks(ref, sem):
        pl.when(in_column)(lambda: await_bytes(ref.at[pl.ds(0, nz - 1)], sem))
        pl.when(jnp.logical_not(in_column))(lambda: await_bytes(ref.at[pl.ds(0, nz)], sem))

    def received(c):
        await_bytes(inbox.at[c], in_sem.at[c])
        return (inbox[c, 0].astype(jnp.float32) + inbox[c, 1].astype(jnp.float32)).astype(jnp.bfloat16)

    def send_back(c):
        q, d = c // nz, lax.rem(c, nz)
        send(carried.at[c], back.at[q, :, mine], back_sent, back_sem, (d, above, to_m))

    def publish(c):
        @pl.when(lax.rem(c, nz) == 0)
        def _():
            await_bytes(slope.at[pl.ds(c, nz)], slope_sem.at[c // nz])

            @pl.when(is_top)
            def _():
                await_blocks(carried, top_sem.at[c // nz])

        @pl.when(jnp.logical_not(is_top))
        def _():
            carried[c] = received(c)

        value = (carried[c].astype(jnp.float32) * slope[c].astype(jnp.float32)).astype(jnp.bfloat16)
        shared[c] = value

        def share(step):
            send(shared.at[c], h.at[c, :, mine], copy_sem.at[c], h_sem.at[c, own // 2], (lax.rem(z + step, nz), s, to_m))

        for step in sorted(range(nz), key=lambda k: -min(k, nz - k)):
            each_other(step, share)

        @pl.when(in_column)
        def _():
            h[c, :, mine] = value

    sources = nz // 2
    nearest = jnp.where(in_column, z, z + 1)

    def multiply(c):
        total = None
        for k in range(sources):
            near = lax.rem(nearest + k, sources)
            if k:
                await_bytes(shared.at[pl.ds(0, 2)], h_sem.at[c, near])
            else:
                pl.when(in_column)(lambda: await_bytes(shared.at[0], h_sem.at[c, near]))
                pl.when(jnp.logical_not(in_column))(lambda: await_bytes(shared.at[pl.ds(0, 2)], h_sem.at[c, near]))
            at = pl.ds(pl.multiple_of(near * 2 * block, 2 * block), 2 * block)
            term = jnp.dot(h[c, :, at], w_t[at, :], preferred_element_type=jnp.float32)
            total = term if total is None else total + term
        for part in range(2):
            value = total[:, part * block : (part + 1) * block]
            value = value + jnp.where(m == part, carried[c].astype(jnp.float32), 0.0)
            product[c, part] = value.astype(jnp.bfloat16)
            send(product.at[c, part], inbox.at[c, m], out_sem.at[c], in_sem.at[c], (z, below, part))

    def advance(i, _):
        @pl.when(i < chunks)
        def _():
            publish(i)

        @pl.when(i >= LAG)
        def _():
            multiply(i - LAG)

        return 0

    lax.fori_loop(0, chunks + LAG, advance, 0)

    @pl.when(jnp.logical_not(is_top))
    def _():
        def later(c, _):
            send_back(c)
            return 0

        lax.fori_loop(0, chunks, later, 0)

    def mix_copy(k):
        at = pl.ds(pl.multiple_of(k * block, block), block)
        return pltpu.make_async_copy(mix.at[:, at], mix_out.at[:, at], mix_sem.at[k])

    def mix_of(k, _):
        at = pl.ds(pl.multiple_of(k * block, block), block)
        value = jnp.dot(x_t[...], h[:, :, at].reshape(chunks * rows, block), preferred_element_type=jnp.float32)
        mix[:, at] = ((chunks * rows) ** (-0.5) * value).astype(jnp.bfloat16)
        mix_copy(k).start()
        return 0

    lax.fori_loop(0, nz, mix_of, 0)

    @pl.when(is_top)
    def _():
        def last(c, _):
            await_bytes(inbox.at[c], out_sem.at[c])
            carried[c] = received(c)
            send_back(c)
            return 0

        lax.fori_loop(0, chunks, last, 0)
        for q in range(micro):
            await_blocks(shared, top_sent.at[q])

    def drain(c, _):
        await_blocks(shared, copy_sem.at[c])

        @pl.when(jnp.logical_not(is_top))
        def _():
            await_bytes(inbox.at[c], out_sem.at[c])

        return 0

    lax.fori_loop(0, chunks, drain, 0)

    @pl.when(jnp.logical_not(at_home))
    def _():
        for q in range(micro):
            await_bytes(slope.at[pl.ds(0, nz)], slope_sent.at[q])

    for k in range(pair):
        for step in steps:
            await_bytes(x.at[0, 0], x_sent.at[k, step])
        for step in range(nz):
            await_bytes(x.at[0, 0], y_sent.at[k, step])
    for k in range(nz):
        mix_copy(k).wait()

    def drain_ring(t, _):
        for q in range(micro):
            await_bytes(sent.at[t, q], ring_sent.at[t, q])
        return 0

    lax.fori_loop(0, nz - 1, drain_ring, 0)

    await_bytes(back, back_sem)
    grad_out[...] = back[...]
    await_bytes(back, back_sent)


def layers(x_own, w, top, cid=0):
    nz = lax.axis_size("dp")
    micro, rows, _ = x_own.shape
    depth, columns = w.shape
    block = columns // nz
    chunks = micro * nz
    dma = pltpu.SemaphoreType.DMA

    def buffer(*shape):
        return pltpu.VMEM(shape, jnp.bfloat16)

    return pl.pallas_call(
        layer_kernel,
        out_shape=(
            jax.ShapeDtypeStruct((depth, columns), jnp.bfloat16),
            jax.ShapeDtypeStruct((micro, rows, columns), jnp.bfloat16),
        ),
        in_specs=[pl.BlockSpec(memory_space=pltpu.VMEM)] * 3,
        out_specs=(
            pl.BlockSpec(memory_space=pl.ANY),
            pl.BlockSpec(memory_space=pltpu.VMEM),
        ),
        scratch_shapes=[
            buffer(micro, nz, rows, depth),
            buffer(depth, chunks * rows),
            buffer(depth, columns),
            buffer(nz - 1, micro, nz * rows, block),
            buffer(nz - 1, micro, nz * rows, block),
            buffer(columns, depth),
            buffer(chunks, rows, block),
            buffer(chunks, rows, columns),
            buffer(chunks, 2, rows, block),
            buffer(chunks, rows, block),
            buffer(chunks, rows, block),
            buffer(chunks, 2, rows, block),
            buffer(chunks, rows, block),
            buffer(micro, rows, columns),
            dma((chunks,)),
            dma((chunks, nz // 2)),
            dma((chunks,)),
            dma((chunks,)),
            dma((nz,)),
            dma,
            dma,
            dma((micro,)),
            dma((micro,)),
            dma((micro,)),
            dma((micro,)),
            dma((micro // 2, nz)),
            dma((micro // 2, nz)),
            dma((micro // 2, nz)),
            dma((micro // 2, nz)),
            dma((micro // 2,)),
            dma((nz - 1, micro)),
            dma((nz - 1, micro)),
        ],
        compiler_params=pltpu.CompilerParams(
            collective_id=cid, has_side_effects=True, vmem_limit_bytes=56 * 1024 * 1024
        ),
        cost_estimate=pl.CostEstimate(
            flops=6 * chunks * rows * depth * columns,
            bytes_accessed=4 * depth * columns,
            transcendentals=0,
        ),
    )(x_own, w, top)


def on_device(stash, w_mix, top_grad, order):
    micro = stash.shape[1]
    weight = w_mix[0]

    series = jnp.arange(micro, dtype=jnp.int32)
    match = (order[0][None, :] == series[:, None]).astype(jnp.int32)
    slot_table = jnp.sum(series[None, :] * match, axis=1)
    x_own = jnp.take(stash[0], slot_table, axis=0)
    grad_mix, input_grad = layers(x_own, weight, top_grad)
    return (input_grad[None], grad_mix[None])


def solution(mesh):
    in_specs = (
        P("section", None, "dp", None),
        P("section", "dp", "mp"),
        P(None, "dp", "mp"),
        P("section", None),
    )
    out_specs = (P("section", None, "dp", "mp"), P("section", "dp", "mp"))
    return jax.shard_map(
        on_device, mesh=mesh, in_specs=in_specs, out_specs=out_specs, check_vma=False
    )
```

```python
import jax
import jax.numpy as jnp
from jax import lax
from jax.experimental import pallas as pl
from jax.experimental.pallas import tpu as pltpu
from jax.sharding import PartitionSpec as P

MESH = pl.DeviceIdType.MESH
LAG = 2
ROWS = 16


def gelu_slope(value):
    inner = 0.7978845608 * (value + 0.044715 * value * value * value)
    tangent = jnp.tanh(inner)
    return 0.5 * (1.0 + tangent) + 0.5 * value * (1.0 - tangent * tangent) * 0.7978845608 * (
        1.0 + 3.0 * 0.044715 * value * value
    )


def send(src, dst, send_sem, recv_sem, device):
    pltpu.make_async_remote_copy(
        src_ref=src, dst_ref=dst, send_sem=send_sem, recv_sem=recv_sem, device_id=device, device_id_type=MESH
    ).start()


def await_bytes(ref, sem):
    pltpu.make_async_copy(ref, ref, sem).wait()


def turn_of(m, nz):
    return (nz // 4) * (1 - 2 * m)


def layer_kernel(x_own, w, top, mix_out, grad_out, x, x_t, mix, ring, sent, w_t, slope_in, h, inbox, carried, shared, product, slope, back, in_sem, h_sem, out_sem, copy_sem, mix_sem, back_sent, back_sem, top_sent, top_sem, slope_sent, slope_sem, x_sem, x_sent, y_sem, y_sent, own_sem, ring_sem, ring_sent):
    nz, ns = lax.axis_size("dp"), lax.axis_size("section")
    z, s, m = lax.axis_index("dp"), lax.axis_index("section"), lax.axis_index("mp")
    chunks, rows, columns = h.shape
    micro, _, whole, depth = x.shape
    per = whole // rows
    share_of = nz * per
    block = columns // nz
    pair = micro // 2
    steps = sorted(range(1, nz), key=lambda k: min(k, nz - k))
    partner = (z, s, 1 - m)
    above, below = lax.rem(s + 1, ns), lax.rem(s + ns - 1, ns)
    is_top = s == ns - 1

    to_m = z // (nz // 2)
    own = 2 * lax.rem(z, nz // 2) + m
    in_column = to_m == m

    def place(number):
        return pl.ds(pl.multiple_of(number * block, block), block)

    def owner_of(number):
        return (m * (nz // 2) + number // 2, s, lax.rem(number, 2))

    def each_other(step, call):
        if step:
            call(step)
        else:
            pl.when(jnp.logical_not(in_column))(lambda: call(step))

    barrier = pltpu.get_barrier_semaphore()

    def greet(device):
        pl.semaphore_signal(barrier, inc=1, device_id=device, device_id_type=MESH)

    for step in range(nz):
        each_other(step, lambda k: greet(owner_of(lax.rem(own + k, nz))))
        each_other(step, lambda k: greet((lax.rem(z + k, nz), s, to_m)))
        greet((m * (nz // 2) + step // 2, below, step % 2))
    for step in steps:
        greet((lax.rem(z + step, nz), s, m))
    greet(partner)
    greet((z, above, 0))
    greet((z, above, 1))
    pl.when(in_column)(lambda: pl.semaphore_wait(barrier, 4 * nz))
    pl.when(jnp.logical_not(in_column))(lambda: pl.semaphore_wait(barrier, 4 * nz + 2))

    mine = place(own)
    number = lax.rem(z + nz + turn_of(m, nz), nz)
    at_home = jnp.logical_and(in_column, number == own)

    batches = [(m if k < pair else 1 - m) * pair + k % pair for k in range(micro)]

    def piece(k, owner):
        return x_own.at[batches[k], :, pl.ds(pl.multiple_of(owner * depth, depth), depth)]

    def own_copy(k):
        return pltpu.make_async_copy(piece(k, z), x.at[batches[k], z], own_sem.at[k])

    for k in range(pair):
        own_copy(k).start()
        for step in steps[::-1]:
            owner = lax.rem(z + step, nz)
            send(piece(k, owner), x.at[batches[k], z], x_sent.at[k, step], x_sem.at[k, step], (owner, s, m))
        send(piece(k, z), x.at[batches[k], z], y_sent.at[k, 0], y_sem.at[k, 0], partner)

    @pl.when(is_top)
    def _():
        def spread(q, _):
            def give(step):
                to = lax.rem(own + step, nz)
                src, dst = top.at[pl.ds(q * per, per), :, place(to)], carried.at[pl.ds((q * nz + z) * per, per)]
                send(src, dst, top_sent.at[q], top_sem.at[q], owner_of(to))

            for step in range(nz):
                each_other(step, give)

            @pl.when(in_column)
            def _():
                carried[pl.ds((q * nz + z) * per, per)] = top[pl.ds(q * per, per), :, mine]

            return 0

        lax.fori_loop(0, micro, spread, 0)

    def transpose(k, _):
        at = pl.ds(pl.multiple_of(k * block, block), block)
        w_t[at, :] = w[:, at].T
        return 0

    lax.fori_loop(0, nz, transpose, 0)

    def partial(t, k):
        owner = lax.rem(z + nz + 1 + t, nz) if k % 2 else lax.rem(z + 2 * nz - 1 - t, nz)
        at = lax.rem(owner + nz + turn_of(m, nz), nz) * block
        return jnp.dot(
            x[batches[k]].reshape(nz * whole, depth),
            w[:, pl.ds(pl.multiple_of(at, block), block)],
            preferred_element_type=jnp.float32,
        )

    def pass_on(t, k, value):
        sent[t, k] = value.astype(jnp.bfloat16)
        to = lax.rem(z + nz - 1, nz) if k % 2 else lax.rem(z + 1, nz)
        send(sent.at[t, k], ring.at[t, k], ring_sent.at[t, k], ring_sem.at[t, k], (to, s, m))

    for k in range(pair):
        own_copy(k).wait()
        for step in steps:
            here = x.at[batches[k], lax.rem(z + nz - step, nz)]
            await_bytes(here, x_sem.at[k, step])
            send(here, here, y_sent.at[k, step], y_sem.at[k, step], partner)
        pass_on(0, k, partial(0, k))
    for k in range(pair, micro):
        for step in range(nz):
            await_bytes(x.at[batches[k], lax.rem(z + nz - step, nz)], y_sem.at[k - pair, step])
        pass_on(0, k, partial(0, k))

    def step_of(t, _):
        @pl.when(t <= 2)
        def _():
            for half in range(pair):
                q = (t - 1) * pair + half
                x_t[:, pl.ds(pl.multiple_of(q * nz * whole, nz * whole), nz * whole)] = x[q].reshape(nz * whole, depth).T

        for k in range(micro):
            value = partial(t, k)
            await_bytes(ring.at[t - 1, k], ring_sem.at[t - 1, k])
            pass_on(t, k, value + ring[t - 1, k].astype(jnp.float32))
        return 0

    lax.fori_loop(1, nz - 1, step_of, 0)

    def local_slope(part, q):
        return pltpu.make_async_copy(slope_in.at[part], slope.at[part], slope_sem.at[q])

    for k in range(micro):
        value = partial(nz - 1, k)
        await_bytes(ring.at[nz - 2, k], ring_sem.at[nz - 2, k])
        value = gelu_slope(value + ring[nz - 2, k].astype(jnp.float32)).astype(jnp.bfloat16)
        q = batches[k]
        part = pl.ds(q * share_of, share_of)
        slope_in[part] = value.reshape(share_of, rows, block)
        pl.when(at_home)(lambda: local_slope(part, q).start())

        @pl.when(jnp.logical_not(at_home))
        def _():
            send(slope_in.at[part], slope.at[part], slope_sent.at[q], slope_sem.at[q], owner_of(number))

    def await_blocks(ref, sem, size=1):
        pl.when(in_column)(lambda: await_bytes(ref.at[pl.ds(0, (nz - 1) * size)], sem))
        pl.when(jnp.logical_not(in_column))(lambda: await_bytes(ref.at[pl.ds(0, nz * size)], sem))

    def received(c):
        await_bytes(inbox.at[c], in_sem.at[c])
        return (inbox[c, 0].astype(jnp.float32) + inbox[c, 1].astype(jnp.float32)).astype(jnp.bfloat16)

    def send_back(c):
        at = c // share_of * per + lax.rem(c, per)
        send(carried.at[c], back.at[at, :, mine], back_sent, back_sem, (lax.rem(c // per, nz), above, to_m))

    def publish(c):
        @pl.when(lax.rem(c, share_of) == 0)
        def _():
            await_bytes(slope.at[pl.ds(c, share_of)], slope_sem.at[c // share_of])

            @pl.when(is_top)
            def _():
                await_blocks(carried, top_sem.at[c // share_of], per)

        @pl.when(jnp.logical_not(is_top))
        def _():
            carried[c] = received(c)

        value = (carried[c].astype(jnp.float32) * slope[c].astype(jnp.float32)).astype(jnp.bfloat16)
        shared[c] = value

        def share(step):
            send(shared.at[c], h.at[c, :, mine], copy_sem.at[c], h_sem.at[c], (lax.rem(z + step, nz), s, to_m))

        for step in sorted(range(nz), key=lambda k: -min(k, nz - k)):
            each_other(step, share)

        @pl.when(in_column)
        def _():
            h[c, :, mine] = value

    def multiply(c):
        await_blocks(shared, h_sem.at[c])
        total = jnp.dot(h[c], w_t[...], preferred_element_type=jnp.float32)
        for part in range(2):
            value = total[:, part * block : (part + 1) * block]
            value = value + jnp.where(m == part, carried[c].astype(jnp.float32), 0.0)
            product[c, part] = value.astype(jnp.bfloat16)
            send(product.at[c, part], inbox.at[c, m], out_sem.at[c], in_sem.at[c], (z, below, part))

    def advance(i, _):
        @pl.when(i < chunks)
        def _():
            publish(i)

        @pl.when(i >= LAG)
        def _():
            multiply(i - LAG)

        return 0

    lax.fori_loop(0, chunks + LAG, advance, 0)

    @pl.when(jnp.logical_not(is_top))
    def _():
        def later(c, _):
            send_back(c)
            return 0

        lax.fori_loop(0, chunks, later, 0)

    def mix_copy(k):
        at = pl.ds(pl.multiple_of(k * block, block), block)
        return pltpu.make_async_copy(mix.at[:, at], mix_out.at[:, at], mix_sem.at[k])

    def mix_of(k, _):
        at = pl.ds(pl.multiple_of(k * block, block), block)
        value = jnp.dot(x_t[...], h[:, :, at].reshape(chunks * rows, block), preferred_element_type=jnp.float32)
        mix[:, at] = ((chunks * rows) ** (-0.5) * value).astype(jnp.bfloat16)
        mix_copy(k).start()
        return 0

    lax.fori_loop(0, nz, mix_of, 0)

    @pl.when(is_top)
    def _():
        def last(c, _):
            await_bytes(inbox.at[c], out_sem.at[c])
            carried[c] = received(c)
            send_back(c)
            return 0

        lax.fori_loop(0, chunks, last, 0)
        for q in range(micro):
            await_blocks(shared, top_sent.at[q], per)

    def drain(c, _):
        await_blocks(shared, copy_sem.at[c])

        @pl.when(jnp.logical_not(is_top))
        def _():
            await_bytes(inbox.at[c], out_sem.at[c])

        return 0

    lax.fori_loop(0, chunks, drain, 0)

    @pl.when(jnp.logical_not(at_home))
    def _():
        for q in range(micro):
            await_bytes(slope.at[pl.ds(0, share_of)], slope_sent.at[q])

    for k in range(pair):
        for step in steps:
            await_bytes(x.at[0, 0], x_sent.at[k, step])
        for step in range(nz):
            await_bytes(x.at[0, 0], y_sent.at[k, step])
    for k in range(nz):
        mix_copy(k).wait()

    def drain_ring(t, _):
        for q in range(micro):
            await_bytes(sent.at[t, q], ring_sent.at[t, q])
        return 0

    lax.fori_loop(0, nz - 1, drain_ring, 0)

    await_bytes(back, back_sem)
    grad_out[...] = back[...]
    await_bytes(back, back_sent)


def layers(x_own, w, top, cid=0):
    nz = lax.axis_size("dp")
    micro, whole, _ = x_own.shape
    rows = min(ROWS, whole)
    per = whole // rows
    depth, columns = w.shape
    block = columns // nz
    chunks = micro * nz * per
    dma = pltpu.SemaphoreType.DMA

    def buffer(*shape):
        return pltpu.VMEM(shape, jnp.bfloat16)

    mix, back = pl.pallas_call(
        layer_kernel,
        out_shape=(
            jax.ShapeDtypeStruct((depth, columns), jnp.bfloat16),
            jax.ShapeDtypeStruct((micro * per, rows, columns), jnp.bfloat16),
        ),
        in_specs=[pl.BlockSpec(memory_space=pltpu.VMEM)] * 3,
        out_specs=(
            pl.BlockSpec(memory_space=pl.ANY),
            pl.BlockSpec(memory_space=pltpu.VMEM),
        ),
        scratch_shapes=[
            buffer(micro, nz, whole, depth),
            buffer(depth, chunks * rows),
            buffer(depth, columns),
            buffer(nz - 1, micro, nz * whole, block),
            buffer(nz - 1, micro, nz * whole, block),
            buffer(columns, depth),
            buffer(chunks, rows, block),
            buffer(chunks, rows, columns),
            buffer(chunks, 2, rows, block),
            buffer(chunks, rows, block),
            buffer(chunks, rows, block),
            buffer(chunks, 2, rows, block),
            buffer(chunks, rows, block),
            buffer(micro * per, rows, columns),
            dma((chunks,)),
            dma((chunks,)),
            dma((chunks,)),
            dma((chunks,)),
            dma((nz,)),
            dma,
            dma,
            dma((micro,)),
            dma((micro,)),
            dma((micro,)),
            dma((micro,)),
            dma((micro // 2, nz)),
            dma((micro // 2, nz)),
            dma((micro // 2, nz)),
            dma((micro // 2, nz)),
            dma((micro // 2,)),
            dma((nz - 1, micro)),
            dma((nz - 1, micro)),
        ],
        compiler_params=pltpu.CompilerParams(
            collective_id=cid, has_side_effects=True, vmem_limit_bytes=56 * 1024 * 1024
        ),
        cost_estimate=pl.CostEstimate(
            flops=6 * chunks * rows * depth * columns,
            bytes_accessed=4 * depth * columns,
            transcendentals=0,
        ),
    )(x_own, w, top.reshape(micro * per, rows, columns))
    return mix, back.reshape(micro, whole, columns)


def on_device(stash, w_mix, top_grad, order):
    micro = stash.shape[1]
    weight = w_mix[0]

    series = jnp.arange(micro, dtype=jnp.int32)
    match = (order[0][None, :] == series[:, None]).astype(jnp.int32)
    slot_table = jnp.sum(series[None, :] * match, axis=1)
    x_own = jnp.take(stash[0], slot_table, axis=0)
    grad_mix, input_grad = layers(x_own, weight, top_grad)
    return (input_grad[None], grad_mix[None])


def solution(mesh):
    in_specs = (
        P("section", None, "dp", None),
        P("section", "dp", "mp"),
        P(None, "dp", "mp"),
        P("section", None),
    )
    out_specs = (P("section", None, "dp", "mp"), P("section", "dp", "mp"))
    return jax.shard_map(
        on_device, mesh=mesh, in_specs=in_specs, out_specs=out_specs, check_vma=False
    )
```

```python
import jax
import jax.numpy as jnp
from jax import lax
from jax.experimental import pallas as pl
from jax.experimental.pallas import tpu as pltpu
from jax.sharding import PartitionSpec as P

MESH = pl.DeviceIdType.MESH
LAG = 2
ROWS = 16


def gelu_slope(value):
    inner = 0.7978845608 * (value + 0.044715 * value * value * value)
    tangent = jnp.tanh(inner)
    return 0.5 * (1.0 + tangent) + 0.5 * value * (1.0 - tangent * tangent) * 0.7978845608 * (
        1.0 + 3.0 * 0.044715 * value * value
    )


def send(src, dst, send_sem, recv_sem, device):
    pltpu.make_async_remote_copy(
        src_ref=src, dst_ref=dst, send_sem=send_sem, recv_sem=recv_sem, device_id=device, device_id_type=MESH
    ).start()


def await_bytes(ref, sem):
    pltpu.make_async_copy(ref, ref, sem).wait()


def turn_of(m, nz):
    return (nz // 4) * (1 - 2 * m)


def layer_kernel(x_own, w, top, mix_out, grad_out, x, x_t, mix, ring, sent, w_t, slope_in, h, inbox, carried, shared, product, slope, back, in_sem, h_sem, out_sem, copy_sem, mix_sem, back_sent, back_sem, top_sent, top_sem, slope_sent, slope_sem, x_sem, x_sent, y_sem, y_sent, own_sem, ring_sem, ring_sent):
    nz, ns = lax.axis_size("dp"), lax.axis_size("section")
    z, s, m = lax.axis_index("dp"), lax.axis_index("section"), lax.axis_index("mp")
    chunks, rows, columns = h.shape
    micro, _, whole, depth = x.shape
    per = whole // rows
    share_of = nz * per
    block = columns // nz
    pair = micro // 2
    steps = sorted(range(1, nz), key=lambda k: min(k, nz - k))
    partner = (z, s, 1 - m)
    above, below = lax.rem(s + 1, ns), lax.rem(s + ns - 1, ns)
    is_top = s == ns - 1

    to_m = z // (nz // 2)
    own = 2 * lax.rem(z, nz // 2) + m
    in_column = to_m == m

    def place(number):
        return pl.ds(pl.multiple_of(number * block, block), block)

    def owner_of(number):
        return (m * (nz // 2) + number // 2, s, lax.rem(number, 2))

    def each_other(step, call):
        if step:
            call(step)
        else:
            pl.when(jnp.logical_not(in_column))(lambda: call(step))

    barrier = pltpu.get_barrier_semaphore()

    def greet(device):
        pl.semaphore_signal(barrier, inc=1, device_id=device, device_id_type=MESH)

    for step in range(nz):
        each_other(step, lambda k: greet(owner_of(lax.rem(own + k, nz))))
        each_other(step, lambda k: greet((lax.rem(z + k, nz), s, to_m)))
        greet((m * (nz // 2) + step // 2, below, step % 2))
    for step in steps:
        greet((lax.rem(z + step, nz), s, m))
    greet(partner)
    greet((z, above, 0))
    greet((z, above, 1))
    pl.when(in_column)(lambda: pl.semaphore_wait(barrier, 4 * nz))
    pl.when(jnp.logical_not(in_column))(lambda: pl.semaphore_wait(barrier, 4 * nz + 2))

    mine = place(own)
    number = lax.rem(z + nz + turn_of(m, nz), nz)
    at_home = jnp.logical_and(in_column, number == own)

    batches = [(m if k < pair else 1 - m) * pair + k % pair for k in range(micro)]

    def piece(k, owner):
        return x_own.at[batches[k], :, pl.ds(pl.multiple_of(owner * depth, depth), depth)]

    def own_copy(k):
        return pltpu.make_async_copy(piece(k, z), x.at[batches[k], z], own_sem.at[k])

    for k in range(pair):
        own_copy(k).start()
        for step in steps[::-1]:
            owner = lax.rem(z + step, nz)
            send(piece(k, owner), x.at[batches[k], z], x_sent.at[k, step], x_sem.at[k, step], (owner, s, m))
        send(piece(k, z), x.at[batches[k], z], y_sent.at[k, 0], y_sem.at[k, 0], partner)

    @pl.when(is_top)
    def _():
        def spread(q, _):
            def give(step):
                to = lax.rem(own + step, nz)
                src, dst = top.at[pl.ds(q * per, per), :, place(to)], carried.at[pl.ds((q * nz + z) * per, per)]
                send(src, dst, top_sent.at[q], top_sem.at[q], owner_of(to))

            for step in range(nz):
                each_other(step, give)

            @pl.when(in_column)
            def _():
                carried[pl.ds((q * nz + z) * per, per)] = top[pl.ds(q * per, per), :, mine]

            return 0

        lax.fori_loop(0, micro, spread, 0)

    def transpose(k, _):
        at = pl.ds(pl.multiple_of(k * block, block), block)
        w_t[at, :] = w[:, at].T
        return 0

    lax.fori_loop(0, nz, transpose, 0)

    def partial(t, k):
        owner = lax.rem(z + nz + 1 + t, nz) if k % 2 else lax.rem(z + 2 * nz - 1 - t, nz)
        at = lax.rem(owner + nz + turn_of(m, nz), nz) * block
        return jnp.dot(
            x[batches[k]].reshape(nz * whole, depth),
            w[:, pl.ds(pl.multiple_of(at, block), block)],
            preferred_element_type=jnp.float32,
        )

    def pass_on(t, k, value):
        sent[t, k] = value.astype(jnp.bfloat16)
        to = lax.rem(z + nz - 1, nz) if k % 2 else lax.rem(z + 1, nz)
        send(sent.at[t, k], ring.at[t, k], ring_sent.at[t, k], ring_sem.at[t, k], (to, s, m))

    for k in range(pair):
        own_copy(k).wait()
        for step in steps:
            here = x.at[batches[k], lax.rem(z + nz - step, nz)]
            await_bytes(here, x_sem.at[k, step])
            send(here, here, y_sent.at[k, step], y_sem.at[k, step], partner)
        pass_on(0, k, partial(0, k))
    for k in range(pair, micro):
        for step in range(nz):
            await_bytes(x.at[batches[k], lax.rem(z + nz - step, nz)], y_sem.at[k - pair, step])
        pass_on(0, k, partial(0, k))

    def step_of(t, _):
        @pl.when(t <= 2)
        def _():
            for half in range(pair):
                q = (t - 1) * pair + half
                x_t[:, pl.ds(pl.multiple_of(q * nz * whole, nz * whole), nz * whole)] = x[q].reshape(nz * whole, depth).T

        for k in range(micro):
            value = partial(t, k)
            await_bytes(ring.at[t - 1, k], ring_sem.at[t - 1, k])
            pass_on(t, k, value + ring[t - 1, k].astype(jnp.float32))
        return 0

    lax.fori_loop(1, nz - 1, step_of, 0)

    def local_slope(part, q):
        return pltpu.make_async_copy(slope_in.at[part], slope.at[part], slope_sem.at[q])

    for k in range(micro):
        value = partial(nz - 1, k)
        await_bytes(ring.at[nz - 2, k], ring_sem.at[nz - 2, k])
        value = gelu_slope(value + ring[nz - 2, k].astype(jnp.float32)).astype(jnp.bfloat16)
        q = batches[k]
        part = pl.ds(q * share_of, share_of)
        slope_in[part] = value.reshape(share_of, rows, block)
        pl.when(at_home)(lambda: local_slope(part, q).start())

        @pl.when(jnp.logical_not(at_home))
        def _():
            send(slope_in.at[part], slope.at[part], slope_sent.at[q], slope_sem.at[q], owner_of(number))

    def await_blocks(ref, sem, size=1):
        pl.when(in_column)(lambda: await_bytes(ref.at[pl.ds(0, (nz - 1) * size)], sem))
        pl.when(jnp.logical_not(in_column))(lambda: await_bytes(ref.at[pl.ds(0, nz * size)], sem))

    def received(c):
        await_bytes(inbox.at[c], in_sem.at[c])
        return (inbox[c, 0].astype(jnp.float32) + inbox[c, 1].astype(jnp.float32)).astype(jnp.bfloat16)

    def send_back(c):
        at = c // share_of * per + lax.rem(c, per)
        send(carried.at[c], back.at[at, :, mine], back_sent, back_sem, (lax.rem(c // per, nz), above, to_m))

    def publish(c):
        @pl.when(lax.rem(c, share_of) == 0)
        def _():
            await_bytes(slope.at[pl.ds(c, share_of)], slope_sem.at[c // share_of])

            @pl.when(is_top)
            def _():
                await_blocks(carried, top_sem.at[c // share_of], per)

        @pl.when(jnp.logical_not(is_top))
        def _():
            carried[c] = received(c)

        value = (carried[c].astype(jnp.float32) * slope[c].astype(jnp.float32)).astype(jnp.bfloat16)
        shared[c] = value

        def share(step):
            send(shared.at[c], h.at[c, :, mine], copy_sem.at[c], h_sem.at[c], (lax.rem(z + step, nz), s, to_m))

        for step in sorted(range(nz), key=lambda k: -min(k, nz - k)):
            each_other(step, share)

        @pl.when(in_column)
        def _():
            h[c, :, mine] = value

    def multiply(c):
        await_blocks(shared, h_sem.at[c])
        total = jnp.dot(h[c], w_t[...], preferred_element_type=jnp.float32)
        for part in range(2):
            value = total[:, part * block : (part + 1) * block]
            value = value + jnp.where(m == part, carried[c].astype(jnp.float32), 0.0)
            product[c, part] = value.astype(jnp.bfloat16)
            send(product.at[c, part], inbox.at[c, m], out_sem.at[c], in_sem.at[c], (z, below, part))

    def settle():
        @pl.when(jnp.logical_not(at_home))
        def _():
            for q in range(micro):
                await_bytes(slope.at[pl.ds(0, share_of)], slope_sent.at[q])

        for k in range(pair):
            for step in steps:
                await_bytes(x.at[0, 0], x_sent.at[k, step])
            for step in range(nz):
                await_bytes(x.at[0, 0], y_sent.at[k, step])
        def drain_ring(t, _):
            for q in range(micro):
                await_bytes(sent.at[t, q], ring_sent.at[t, q])
            return 0

        lax.fori_loop(0, nz - 1, drain_ring, 0)

    pl.when(jnp.logical_not(is_top))(settle)

    def advance(i, _):
        @pl.when(i < chunks)
        def _():
            publish(i)

        @pl.when(i >= LAG)
        def _():
            multiply(i - LAG)

        return 0

    lax.fori_loop(0, chunks + LAG, advance, 0)

    @pl.when(jnp.logical_not(is_top))
    def _():
        def later(j, _):
            src, dst = carried.at[pl.ds(j * per, per)], back.at[pl.ds(j // nz * per, per), :, mine]
            send(src, dst, back_sent, back_sem, (lax.rem(j, nz), above, to_m))
            return 0

        lax.fori_loop(0, chunks // per, later, 0)

    def mix_copy(k):
        at = pl.ds(pl.multiple_of(k * block, block), block)
        return pltpu.make_async_copy(mix.at[:, at], mix_out.at[:, at], mix_sem.at[k])

    def mix_of(k, _):
        at = pl.ds(pl.multiple_of(k * block, block), block)
        value = jnp.dot(x_t[...], h[:, :, at].reshape(chunks * rows, block), preferred_element_type=jnp.float32)
        mix[:, at] = ((chunks * rows) ** (-0.5) * value).astype(jnp.bfloat16)
        mix_copy(k).start()
        return 0

    lax.fori_loop(0, nz, mix_of, 0)

    @pl.when(is_top)
    def _():
        def last(c, _):
            await_bytes(inbox.at[c], out_sem.at[c])
            carried[c] = received(c)
            send_back(c)
            return 0

        lax.fori_loop(0, chunks, last, 0)
        for q in range(micro):
            await_blocks(shared, top_sent.at[q], per)

    def drain(c, _):
        await_blocks(shared, copy_sem.at[c])

        @pl.when(jnp.logical_not(is_top))
        def _():
            await_bytes(inbox.at[c], out_sem.at[c])

        return 0

    lax.fori_loop(0, chunks, drain, 0)

    pl.when(is_top)(settle)
    for k in range(nz):
        mix_copy(k).wait()

    await_bytes(back, back_sem)
    grad_out[...] = back[...]
    await_bytes(back, back_sent)


def layers(x_own, w, top, cid=0):
    nz = lax.axis_size("dp")
    micro, whole, _ = x_own.shape
    rows = min(ROWS, whole)
    per = whole // rows
    depth, columns = w.shape
    block = columns // nz
    chunks = micro * nz * per
    dma = pltpu.SemaphoreType.DMA

    def buffer(*shape):
        return pltpu.VMEM(shape, jnp.bfloat16)

    mix, back = pl.pallas_call(
        layer_kernel,
        out_shape=(
            jax.ShapeDtypeStruct((depth, columns), jnp.bfloat16),
            jax.ShapeDtypeStruct((micro * per, rows, columns), jnp.bfloat16),
        ),
        in_specs=[pl.BlockSpec(memory_space=pltpu.VMEM)] * 3,
        out_specs=(
            pl.BlockSpec(memory_space=pl.ANY),
            pl.BlockSpec(memory_space=pltpu.VMEM),
        ),
        scratch_shapes=[
            buffer(micro, nz, whole, depth),
            buffer(depth, chunks * rows),
            buffer(depth, columns),
            buffer(nz - 1, micro, nz * whole, block),
            buffer(nz - 1, micro, nz * whole, block),
            buffer(columns, depth),
            buffer(chunks, rows, block),
            buffer(chunks, rows, columns),
            buffer(chunks, 2, rows, block),
            buffer(chunks, rows, block),
            buffer(chunks, rows, block),
            buffer(chunks, 2, rows, block),
            buffer(chunks, rows, block),
            buffer(micro * per, rows, columns),
            dma((chunks,)),
            dma((chunks,)),
            dma((chunks,)),
            dma((chunks,)),
            dma((nz,)),
            dma,
            dma,
            dma((micro,)),
            dma((micro,)),
            dma((micro,)),
            dma((micro,)),
            dma((micro // 2, nz)),
            dma((micro // 2, nz)),
            dma((micro // 2, nz)),
            dma((micro // 2, nz)),
            dma((micro // 2,)),
            dma((nz - 1, micro)),
            dma((nz - 1, micro)),
        ],
        compiler_params=pltpu.CompilerParams(
            collective_id=cid, has_side_effects=True, vmem_limit_bytes=56 * 1024 * 1024
        ),
        cost_estimate=pl.CostEstimate(
            flops=6 * chunks * rows * depth * columns,
            bytes_accessed=4 * depth * columns,
            transcendentals=0,
        ),
    )(x_own, w, top.reshape(micro * per, rows, columns))
    return mix, back.reshape(micro, whole, columns)


def on_device(stash, w_mix, top_grad, order):
    micro = stash.shape[1]
    weight = w_mix[0]

    series = jnp.arange(micro, dtype=jnp.int32)
    match = (order[0][None, :] == series[:, None]).astype(jnp.int32)
    slot_table = jnp.sum(series[None, :] * match, axis=1)
    x_own = jnp.take(stash[0], slot_table, axis=0)
    grad_mix, input_grad = layers(x_own, weight, top_grad)
    return (input_grad[None], grad_mix[None])


def solution(mesh):
    in_specs = (
        P("section", None, "dp", None),
        P("section", "dp", "mp"),
        P(None, "dp", "mp"),
        P("section", None),
    )
    out_specs = (P("section", None, "dp", "mp"), P("section", "dp", "mp"))
    return jax.shard_map(
        on_device, mesh=mesh, in_specs=in_specs, out_specs=out_specs, check_vma=False
    )
```
